32 devices in a mesh: dp: 8 (over z, x), tensor: 4 (over y, core).
Axes of the slice: x: 2, y: 2, z: 4, core: 2. Of those that a mesh axis runs over, the one named last changes fastest.
Arguments:
- inputs: bfloat16 [8192, 1024], P(('dp', 'tensor')), may hold values from -6 to 6
- cotangent: bfloat16 [8192, 1024], P(('dp', 'tensor')), may hold values from -6 to 6
- gain_in: bfloat16 [1024], P('dp'), may hold values from 0.5 to 1.5
- query_weight: bfloat16 [1024, 512], P('dp', 'tensor'), may hold values from -0.1875 to 0.1875
- shared_matrix: bfloat16 [1024, 512], P('dp'), may hold values from -0.1875 to 0.1875
- attention_out: bfloat16 [1024, 512], P('dp', 'tensor'), may hold values from -2 to 2
- mixer_in: bfloat16 [1024, 2, 1536], P('dp', None, 'tensor'), may hold values from -0.1875 to 0.1875
- step_weight: bfloat16 [1024, 24], P('dp', 'tensor'), may hold values from -0.1875 to 0.1875
- filter_inner: bfloat16 [5, 1536], P(None, 'tensor'), may hold values from -3 to 3
- filter_state: bfloat16 [256, 5], P('dp'), may hold values from -3 to 3
- step_bias: bfloat16 [24], P('tensor'), may hold values from -4 to -1
- log_decay: bfloat16 [24], P('tensor'), may hold values from -7 to 2.796875
- skip_gain: bfloat16 [24], P('tensor'), may hold values from 0.5 to 1.5
- mixer_gain: bfloat16 [1536], P('tensor'), may hold values from 0.5 to 1.5
- mixer_out: bfloat16 [1024, 1536], P('dp', 'tensor'), may hold values from -0.15625 to 0.15625
- gain_post: bfloat16 [1024], P('dp'), may hold values from 0.5 to 1.5
- gate_up: bfloat16 [1024, 2, 2048], P('dp', None, 'tensor'), may hold values from -0.1875 to 0.1875
- down_weight: bfloat16 [1024, 2048], P('dp', 'tensor'), may hold values from -0.125 to 0.125
Outputs:
- output: bfloat16 [8192, 1024], P(('dp', 'tensor'))
- back_inputs: float32 [8192, 1024], P(('dp', 'tensor'))
- back_gain_in: float32 [1024], P('dp')
- back_query: float32 [1024, 512], P('dp', 'tensor')
- back_shared: float32 [1024, 512], P('dp')
- back_attention: float32 [1024, 512], P('dp', 'tensor')
- back_mixer_in: float32 [1024, 2, 1536], P('dp', None, 'tensor')
- back_step: float32 [1024, 24], P('dp', 'tensor')
- back_filter_inner: float32 [5, 1536], P(None, 'tensor')
- back_filter_state: float32 [256, 5], P('dp')
- back_step_bias: float32 [24], P('tensor')
- back_log_decay: float32 [24], P('tensor')
- back_skip_gain: float32 [24], P('tensor')
- back_mixer_gain: float32 [1536], P('tensor')
- back_mixer_out: float32 [1024, 1536], P('dp', 'tensor')
- back_gain_post: float32 [1024], P('dp')
- back_gate_up: float32 [1024, 2, 2048], P('dp', None, 'tensor')
- back_down: float32 [1024, 2048], P('dp', 'tensor')
The draws below stay inside these ranges and needn't reach their ends.
All inputs are finite; a program needn't handle non-finite values.
Results may differ from the reference program's by a relative error of at most 0.03.
Values may be sent and summed in bfloat16 or wider, within the bound.
A program may use at most 192 MiB of HBM per device.

```python
import jax
import jax.numpy as jnp
from jax import lax

MODEL_WIDTH = 1024
QUERY_HEADS = 8
HEAD_SIZE = 64
KEY_VALUE_HEADS = 2
NH = 24
STATE_SIZE = 128
FF = 2048
KCONV = 4
SEQ = 1024
BLK = 128
DSSM = 1536
TOKENS = 8192
N_DP = 8
N_TENSOR = 4


def strengthened(values, key, source, target, parts, factor):
    def block_of(dim):
        return (jnp.arange(values.shape[dim]) // (values.shape[dim] // parts)).reshape((-1,) + (1,) * (values.ndim - 1 - dim))

    one_side = jax.random.permutation(key, parts)[block_of(target)]
    other_side = (block_of(target) + parts // 2) % parts
    return jnp.where((block_of(source) == one_side) | (block_of(source) == other_side), factor * values, values)


def block_levels(stream_key, shape, shards, smallest, largest):
    level = 1.0
    for dim, blocks in shards:
        steps = jax.random.uniform(jax.random.fold_in(jax.random.fold_in(stream_key, 6), dim), (blocks,), jnp.float32, smallest / len(shards), largest / len(shards))
        level = level * jnp.repeat(jnp.exp(steps), shape[dim] // blocks).reshape((-1,) + (1,) * (len(shape) - 1 - dim))
    return level


def centred(rng, shape, scale, most, cuts=(), kind=jnp.bfloat16):
    values = jax.random.normal(rng, shape, jnp.float32) * scale
    if len(cuts) > 0:
        values = block_levels(rng, shape, cuts, -0.22, 0.18) * values
    return jnp.clip(values, min=-most, max=most).astype(kind)


def heavy_noise(rng, shape, scale, bound, cuts, heavy, kind=jnp.bfloat16):
    drawn = scale * jax.random.normal(rng, shape, jnp.float32)
    if cuts:
        drawn = drawn * block_levels(rng, shape, cuts, -0.22, 0.18)
    return jnp.clip(strengthened(drawn, jax.random.fold_in(rng, 3), *heavy), -bound, bound).astype(kind)


def setup_inputs(seed: int = 0) -> dict:
    keys = jax.random.split(jax.random.key(seed), 19)
    inputs = centred(keys[0], (TOKENS, MODEL_WIDTH), 1.0, 6.0, ((0, 32),))
    cotangent = heavy_noise(keys[1], (TOKENS, MODEL_WIDTH), 1.0, 6.0, ((0, 32),), (0, 1, 32, 2.75))
    gain_in = jnp.clip(1.0 + 0.1 * jax.random.normal(keys[2], (MODEL_WIDTH,), jnp.float32), 0.5, 1.5).astype(jnp.bfloat16)
    query_weight = centred(keys[3], (MODEL_WIDTH, QUERY_HEADS * HEAD_SIZE), MODEL_WIDTH ** -0.5, 0.1875, ((0, 8), (1, 4)))
    shared_matrix = centred(keys[4], (MODEL_WIDTH, 2 * KEY_VALUE_HEADS * HEAD_SIZE + 2 * STATE_SIZE), MODEL_WIDTH ** -0.5, 0.1875, ((0, 8),))
    attention_out = centred(keys[5], (MODEL_WIDTH, QUERY_HEADS * HEAD_SIZE), (QUERY_HEADS * HEAD_SIZE // 64) ** -0.5, 2.0, ((0, 8), (1, 4)))
    mixer_in = centred(keys[6], (MODEL_WIDTH, 2, DSSM), MODEL_WIDTH ** -0.5, 0.1875, ((0, 8), (2, 4)))
    step_weight = centred(keys[7], (MODEL_WIDTH, NH), MODEL_WIDTH ** -0.5, 0.1875, ((0, 8), (1, 4)))
    filter_inner = centred(keys[8], (KCONV + 1, DSSM), KCONV ** -0.5, 3.0, ((1, 4),))
    filter_state = centred(keys[9], (2 * STATE_SIZE, KCONV + 1), KCONV ** -0.5, 3.0, ((0, 8),))
    step_bias = jnp.clip(-4.0 + 3.0 * jax.random.uniform(keys[10], (NH,), jnp.float32) ** block_levels(keys[10], (NH,), ((0, 4),), -0.2, 0.2), -4.0, -1.0).astype(jnp.bfloat16)
    log_decay = jnp.clip(-7.0 + 9.796875 * jax.random.uniform(keys[11], (NH,), jnp.float32) ** block_levels(keys[11], (NH,), ((0, 4),), -0.2, 0.2), -7.0, 2.796875).astype(jnp.bfloat16)
    skip_gain = jnp.clip(0.5 + 1.0 * jax.random.uniform(keys[12], (NH,), jnp.float32) ** block_levels(keys[12], (NH,), ((0, 4),), -0.2, 0.2), 0.5, 1.5).astype(jnp.bfloat16)
    mixer_gain = jnp.clip(1.0 + 0.1 * jax.random.normal(keys[13], (DSSM,), jnp.float32), 0.5, 1.5).astype(jnp.bfloat16)
    mixer_out = centred(keys[14], (MODEL_WIDTH, DSSM), DSSM ** -0.5, 0.15625, ((0, 8), (1, 4)))
    gain_post = jnp.clip(1.0 + 0.1 * jax.random.normal(keys[15], (MODEL_WIDTH,), jnp.float32), 0.5, 1.5).astype(jnp.bfloat16)
    gate_up = centred(keys[16], (MODEL_WIDTH, 2, FF), MODEL_WIDTH ** -0.5, 0.1875, ((0, 8), (2, 4)))
    down_weight = centred(keys[17], (MODEL_WIDTH, FF), FF ** -0.5, 0.125, ((0, 8), (1, 4)))
    return dict(inputs=inputs, cotangent=cotangent, gain_in=gain_in, query_weight=query_weight, shared_matrix=shared_matrix, attention_out=attention_out, mixer_in=mixer_in, step_weight=step_weight, filter_inner=filter_inner, filter_state=filter_state, step_bias=step_bias, log_decay=log_decay, skip_gain=skip_gain, mixer_gain=mixer_gain, mixer_out=mixer_out, gain_post=gain_post, gate_up=gate_up, down_weight=down_weight)


epsilon = 1e-05
rope_base = 100000000000.0
highest_precision = lax.Precision.HIGHEST

@jax.custom_vjp
def reduced_dtype(v):
    return lax.optimization_barrier(v.astype(jnp.bfloat16)).astype(jnp.float32)

@jax.custom_vjp
def low_back(v):
    return v

def low_keep(v):
    return (reduced_dtype(v), None)

def low_pass(kept, grad):
    return (grad,)

def back_keep(v):
    return (v, None)

def back_low(kept, grad):
    return (reduced_dtype(grad),)
reduced_dtype.defvjp(low_keep, low_pass)
low_back.defvjp(back_keep, back_low)

def product(left, right):
    return jnp.dot(left, right, precision=highest_precision)

def norm_scale(values):
    return lax.rsqrt(lax.optimization_barrier(jnp.mean(values * values, axis=-1, keepdims=True)) + epsilon)

def rotary_embed(values, sequence_length, sign):
    half = values.shape[-1] // 2
    position = jnp.arange(sequence_length, dtype=jnp.float32)
    frequency = rope_base ** (-jnp.arange(half, dtype=jnp.float32) * 2.0 / values.shape[-1])
    angle = position[:, None] * frequency[None, :]
    cosine = jnp.cos(angle)[:, None, :]
    sine = sign * jnp.sin(angle)[:, None, :]
    first = values[..., :half]
    second = values[..., half:]
    return jnp.concatenate([first * cosine - second * sine, second * cosine + first * sine], axis=-1)

def causal_filter(values, taps, bias):
    width = taps.shape[0]
    sequence_length = values.shape[0]
    padded = jnp.pad(values, ((width - 1, 0), (0, 0)))
    total = bias[None, :] + jnp.zeros_like(values)
    for offset in range(width):
        total = total + taps[offset][None, :] * padded[offset:offset + sequence_length]
    return total

def mixer_input(inner_raw, state_raw, step_raw, filter_inner, filter_state, step_bias):
    kernel = filter_inner.shape[0] - 1
    inner = jax.nn.silu(causal_filter(inner_raw, filter_inner[:kernel], filter_inner[kernel]))
    state_in = jax.nn.silu(causal_filter(state_raw, jnp.transpose(filter_state[:, :kernel]), filter_state[:, kernel]))
    step_size = jax.nn.softplus(step_raw + step_bias[None, :])
    return (inner, state_in, step_size)

def state_scan(inner, state_in, step_size, gate_z, log_decay, skip_gain, block):
    sequence_length, channels = inner.shape
    heads = step_size.shape[1]
    head = channels // heads
    state_width = state_in.shape[1] // 2
    count = sequence_length // block
    inner_blocks = inner.reshape(count, block, heads, head)
    state_input_keys = state_in[:, :state_width].reshape(count, block, state_width)
    state_output_reads = state_in[:, state_width:].reshape(count, block, state_width)
    rate = step_size * (-jnp.exp(log_decay))[None, :]
    running = jnp.cumsum(rate.reshape(count, block, heads), axis=1)
    step_blocks = step_size.reshape(count, block, heads)
    within_group = jnp.einsum('xfw,xkw->xfk', state_output_reads, state_input_keys, precision=highest_precision)
    lower = jnp.arange(block)[:, None] >= jnp.arange(block)[None, :]
    spread = running[:, :, None, :] - running[:, None, :, :]
    decay = jnp.exp(jnp.where(lower[None, :, :, None], spread, -1e+30))
    mixing = within_group[..., None] * decay * step_blocks[:, None, :, :]
    local_out = jnp.einsum('clrh,crhp->clhp', mixing, inner_blocks, precision=highest_precision)
    tail = jnp.exp(running[:, -1:, :] - running) * step_blocks
    block_state = jnp.einsum('crh,crhp,crn->chpn', tail, inner_blocks, state_input_keys, precision=highest_precision)
    total_decay = jnp.exp(running[:, -1, :])

    def advance(carry, pieces):
        fade, fresh = pieces
        return (carry * fade[:, None, None] + fresh, carry)
    zero_state = jnp.zeros((heads, head, state_width), inner.dtype)
    final, entering = lax.scan(advance, zero_state, (total_decay, block_state))
    carried = jnp.einsum('cln,chpn->clhp', state_output_reads, entering, precision=highest_precision) * jnp.exp(running)[..., None]
    result = (local_out + carried).reshape(sequence_length, channels) + inner * jnp.repeat(skip_gain, head)[None, :]
    return result * jax.nn.silu(gate_z)

def layer(inputs, params):
    gain_in, query_weight, shared_matrix, attention_out, mixer_in, step_weight, filter_inner, filter_state, step_bias, log_decay, skip_gain, mixer_gain, mixer_out, gain_post, gate_up, down_weight = params
    sequence_length = inputs.shape[0]
    key_value_width = KEY_VALUE_HEADS * HEAD_SIZE
    normed_in = reduced_dtype(inputs * norm_scale(inputs) * gain_in)
    query = low_back(product(normed_in, query_weight))
    shared_projection = low_back(product(normed_in, shared_matrix))
    query_low = reduced_dtype(rotary_embed(query.reshape(sequence_length, QUERY_HEADS, HEAD_SIZE), sequence_length, 1.0))
    keys_reduced = reduced_dtype(rotary_embed(shared_projection[:, :key_value_width].reshape(sequence_length, KEY_VALUE_HEADS, HEAD_SIZE), sequence_length, 1.0))
    values_reduced = reduced_dtype(shared_projection[:, key_value_width:2 * key_value_width].reshape(sequence_length, KEY_VALUE_HEADS, HEAD_SIZE))
    head_group = QUERY_HEADS // KEY_VALUE_HEADS
    keys_all = jnp.repeat(keys_reduced, head_group, axis=1)
    values_all = jnp.repeat(values_reduced, head_group, axis=1)
    scores = low_back(jnp.einsum('qhd,khd->hqk', query_low, keys_all, precision=highest_precision) * HEAD_SIZE ** (-0.5))
    visible = jnp.arange(sequence_length)[:, None] >= jnp.arange(sequence_length)[None, :]
    scores = jnp.where(visible[None], scores, -1e+30)
    shares_low = reduced_dtype(jax.nn.softmax(scores, axis=-1))
    mixed = jnp.einsum('hqk,khd->qhd', shares_low, values_all, precision=highest_precision).reshape(sequence_length, QUERY_HEADS * HEAD_SIZE)
    mixed = low_back(reduced_dtype(mixed))
    mixer_raw = low_back(jnp.einsum('sd,dcf->scf', normed_in, mixer_in, precision=highest_precision))
    step_raw = low_back(product(normed_in, step_weight))
    inner, state_in, step_size = mixer_input(mixer_raw[:, 1], shared_projection[:, 2 * key_value_width:], step_raw, filter_inner, filter_state, step_bias)
    gated = state_scan(reduced_dtype(inner), reduced_dtype(state_in), step_size, mixer_raw[:, 0], log_decay, skip_gain, BLK)
    mixer_low = reduced_dtype(gated * norm_scale(gated) * mixer_gain)
    attention_width = QUERY_HEADS * HEAD_SIZE // N_TENSOR
    mixer_width = DSSM // N_TENSOR
    ffn_width = FF // N_TENSOR
    branch_total = jnp.zeros_like(inputs)
    for shard in range(N_TENSOR):
        att_cols = slice(shard * attention_width, (shard + 1) * attention_width)
        mix_cols = slice(shard * mixer_width, (shard + 1) * mixer_width)
        piece = product(mixed[:, att_cols], jnp.transpose(attention_out[:, att_cols])) + product(mixer_low[:, mix_cols], jnp.transpose(mixer_out[:, mix_cols]))
        branch_total = branch_total + reduced_dtype(piece)
    hidden = inputs + low_back(branch_total)
    normed_post = reduced_dtype(hidden * norm_scale(hidden) * gain_post)
    gate_values = low_back(jnp.einsum('sd,dcf->scf', normed_post, gate_up, precision=highest_precision))
    activated = reduced_dtype(jax.nn.silu(gate_values[:, 0]) * gate_values[:, 1])
    ffn_total = jnp.zeros_like(inputs)
    for shard in range(N_TENSOR):
        ffn_cols = slice(shard * ffn_width, (shard + 1) * ffn_width)
        ffn_total = ffn_total + reduced_dtype(product(activated[:, ffn_cols], jnp.transpose(down_weight[:, ffn_cols])))
    return hidden + ffn_total

def reference(inputs, cotangent, gain_in, query_weight, shared_matrix, attention_out, mixer_in, step_weight, filter_inner, filter_state, step_bias, log_decay, skip_gain, mixer_gain, mixer_out, gain_post, gate_up, down_weight):
    params = tuple((piece.astype(jnp.float32) for piece in (gain_in, query_weight, shared_matrix, attention_out, mixer_in, step_weight, filter_inner, filter_state, step_bias, log_decay, skip_gain, mixer_gain, mixer_out, gain_post, gate_up, down_weight)))
    seq_inputs = inputs.astype(jnp.float32).reshape(N_DP, SEQ, MODEL_WIDTH)
    seq_back = cotangent.astype(jnp.float32).reshape(N_DP, SEQ, MODEL_WIDTH)
    zero_grads = tuple((jnp.zeros_like(piece) for piece in params))

    def one_sequence(totals, pieces):
        rows, back_rows = pieces
        result, back_fn = jax.vjp(layer, rows, params)
        back_x, back_params = back_fn(back_rows)
        totals = tuple((left + right for left, right in zip(totals, back_params)))
        return (totals, (result, back_x))
    totals, (results, back_x) = lax.scan(one_sequence, zero_grads, (seq_inputs, seq_back))
    t_gain_in, t_query, t_shared, t_attention, t_mixer_in, t_step, t_filter_inner, t_filter_state, t_step_bias, t_log_decay, t_skip_gain, t_mixer_gain, t_mixer_out, t_gain_post, t_gate_up, t_down = totals
    return (results.reshape(TOKENS, MODEL_WIDTH).astype(jnp.bfloat16), back_x.reshape(TOKENS, MODEL_WIDTH), t_gain_in, t_query, t_shared, t_attention, t_mixer_in, t_step, t_filter_inner, t_filter_state, t_step_bias, t_log_decay, t_skip_gain, t_mixer_gain, t_mixer_out, t_gain_post, t_gate_up, t_down)
```

```python
import jax
import jax.numpy as jnp
from jax import lax
from jax.sharding import PartitionSpec as P

QUERY_HEADS = 8
HEAD_SIZE = 64
KEY_VALUE_HEADS = 2
NH = 24
PH = 64
BLK = 128
QB = 512


epsilon = 1e-05
rope_base = 100000000000.0
highest_precision = lax.Precision.HIGHEST


def as_sent(x):

    def short(part):
        return part.astype(jnp.bfloat16) if part.dtype == jnp.float32 else part

    return jax.tree.map(short, x)


def norm_scale(values):
    return lax.rsqrt(jnp.mean(values * values, axis=-1, keepdims=True) + epsilon)


def rotary_embed(values, sequence_length, sign):
    half = values.shape[-1] // 2
    position = jnp.arange(sequence_length, dtype=jnp.float32)
    frequency = rope_base ** (-jnp.arange(half, dtype=jnp.float32) * 2.0 / values.shape[-1])
    angle = position[:, None] * frequency[None, :]
    cosine = jnp.cos(angle)[:, None, :]
    sine = sign * jnp.sin(angle)[:, None, :]
    first = values[..., :half]
    second = values[..., half:]
    return jnp.concatenate(
        [first * cosine - second * sine, second * cosine + first * sine], axis=-1
    )


def causal_filter(values, taps, bias):
    width = taps.shape[0]
    sequence_length = values.shape[0]
    padded = jnp.pad(values, ((width - 1, 0), (0, 0)))
    total = bias[None, :] + jnp.zeros_like(values)
    for offset in range(width):
        total = total + taps[offset][None, :] * padded[offset : offset + sequence_length]
    return total


def mixer_input(inner_raw, state_raw, step_raw, filter_inner, filter_state, step_bias):
    kernel = filter_inner.shape[0] - 1
    inner = jax.nn.silu(causal_filter(inner_raw, filter_inner[:kernel], filter_inner[kernel]))
    state_in = jax.nn.silu(
        causal_filter(state_raw, jnp.transpose(filter_state[:, :kernel]), filter_state[:, kernel])
    )
    step_size = jax.nn.softplus(step_raw + step_bias[None, :])
    return (inner, state_in, step_size)


def state_scan(inner, state_in, step_size, gate_z, log_decay, skip_gain, block):
    sequence_length, channels = inner.shape
    heads = step_size.shape[1]
    head = channels // heads
    state_width = state_in.shape[1] // 2
    count = sequence_length // block
    inner_blocks = inner.reshape(count, block, heads, head)
    state_input_keys = state_in[:, :state_width].reshape(count, block, state_width)
    state_output_reads = state_in[:, state_width:].reshape(count, block, state_width)
    rate = step_size * (-jnp.exp(log_decay))[None, :]
    running = jnp.cumsum(rate.reshape(count, block, heads), axis=1)
    step_blocks = step_size.reshape(count, block, heads)
    within_group = jnp.einsum(
        "xfw,xkw->xfk", state_output_reads, state_input_keys, precision=highest_precision
    )
    lower = jnp.arange(block)[:, None] >= jnp.arange(block)[None, :]
    spread = running[:, :, None, :] - running[:, None, :, :]
    decay = jnp.exp(jnp.where(lower[None, :, :, None], spread, -1e30))
    mixing = within_group[..., None] * decay * step_blocks[:, None, :, :]
    local_out = jnp.einsum("clrh,crhp->clhp", mixing, inner_blocks, precision=highest_precision)
    tail = jnp.exp(running[:, -1:, :] - running) * step_blocks
    block_state = jnp.einsum(
        "crh,crhp,crn->chpn", tail, inner_blocks, state_input_keys, precision=highest_precision
    )
    total_decay = jnp.exp(running[:, -1, :])

    carry = jnp.zeros((heads, head, state_width), inner.dtype)
    states = []
    for index in range(count):
        states.append(carry)
        carry = carry * total_decay[index][:, None, None] + block_state[index]
    entering = jnp.stack(states)
    carried = (
        jnp.einsum("cln,chpn->clhp", state_output_reads, entering, precision=highest_precision)
        * jnp.exp(running)[..., None]
    )
    result = (local_out + carried).reshape(sequence_length, channels) + inner * jnp.repeat(
        skip_gain, head
    )[None, :]
    return result * jax.nn.silu(gate_z)


def attend(query_low, keys_reduced, values_reduced, block):
    sequence_length, heads, head = query_low.shape
    scale = head ** (-0.5)
    parts = []
    totals = []
    for start in range(0, sequence_length, block):
        end = start + block
        rows = query_low[start:end]
        scores = (
            jnp.einsum("qhd,kd->hqk", rows, keys_reduced[:end], preferred_element_type=jnp.float32)
            * scale
        )
        visible = (start + jnp.arange(block))[:, None] >= jnp.arange(end)[None, :]
        scores = jnp.where(visible[None], scores, -1e30)
        peak = jnp.max(scores, axis=-1, keepdims=True)
        weights = jnp.exp(scores - peak)
        total = jnp.sum(weights, axis=-1, keepdims=True)
        shares_low = (weights / total).astype(jnp.bfloat16)
        parts.append(
            jnp.einsum(
                "hqk,kd->qhd", shares_low, values_reduced[:end], preferred_element_type=jnp.float32
            ).reshape(block, heads * head)
        )
        totals.append(peak + jnp.log(total))
    return (jnp.concatenate(parts, axis=0), totals)


def attend_back(query_low, keys_reduced, values_reduced, totals, back_mixed_low, block):
    sequence_length, heads, head = query_low.shape
    scale = head ** (-0.5)
    back_view = back_mixed_low.reshape(sequence_length, heads, head)
    back_keys = jnp.zeros((sequence_length, head), jnp.float32)
    back_values = jnp.zeros((sequence_length, head), jnp.float32)
    queries = []
    for index, start in enumerate(range(0, sequence_length, block)):
        end = start + block
        rows = query_low[start:end]
        back_rows = back_view[start:end]
        scores = (
            jnp.einsum("qhd,kd->hqk", rows, keys_reduced[:end], preferred_element_type=jnp.float32)
            * scale
        )
        visible = (start + jnp.arange(block))[:, None] >= jnp.arange(end)[None, :]
        shares = jnp.where(visible[None], jnp.exp(jnp.where(visible[None], scores - totals[index], -1e30)), 0.0)
        back_shares = jnp.einsum(
            "qhd,kd->hqk", back_rows, values_reduced[:end], preferred_element_type=jnp.float32
        )
        inner = jnp.sum(shares * back_shares, axis=-1, keepdims=True)
        back_scores = (shares * (back_shares - inner)).astype(jnp.bfloat16)
        queries.append(
            jnp.einsum(
                "hqk,kd->qhd", back_scores, keys_reduced[:end], preferred_element_type=jnp.float32
            )
            * scale
        )
        rest = ((0, sequence_length - end), (0, 0))
        back_keys = back_keys + jnp.pad(
            jnp.einsum("hqk,qhd->kd", back_scores, rows, preferred_element_type=jnp.float32)
            * scale,
            rest,
        )
        back_values = back_values + jnp.pad(
            jnp.einsum(
                "hqk,qhd->kd",
                shares.astype(jnp.bfloat16),
                back_rows,
                preferred_element_type=jnp.float32,
            ),
            rest,
        )
    return (jnp.concatenate(queries, axis=0), back_keys, back_values)


def gather_rows(values):
    return lax.all_gather(values, "tensor", axis=0, tiled=True)


def scatter_rows(values):
    return lax.psum_scatter(values, "tensor", scatter_dimension=0, tiled=True).astype(jnp.float32)


def scatter_grads(values):
    return jax.tree.map(
        lambda part: part.astype(jnp.float32),
        lax.psum_scatter(as_sent(values), "tensor", scatter_dimension=0, tiled=True),
    )


def body(
    inputs,
    cotangent,
    gain_in,
    query_weight,
    shared_matrix,
    attention_out,
    mixer_in,
    step_weight,
    filter_inner,
    filter_state,
    step_bias,
    log_decay,
    skip_gain,
    mixer_gain,
    mixer_out,
    gain_post,
    gate_up,
    down_weight,
):
    tensor_position = lax.axis_index("tensor")
    bf16 = jnp.bfloat16
    f32 = jnp.float32

    def dot(left, right):
        return jnp.dot(left, right, preferred_element_type=f32)

    def dot_t(left, right):
        return lax.dot_general(left, right, (((1,), (1,)), ((), ())), preferred_element_type=f32)

    def t_dot(left, right):
        return lax.dot_general(left, right, (((0,), (0,)), ((), ())), preferred_element_type=f32)

    own_rows = query_weight.shape[0]
    width = inputs.shape[1]
    dp_count = width // own_rows
    query_width = query_weight.shape[1]
    shared_width = shared_matrix.shape[1]
    channels = mixer_in.shape[2]
    hidden_units = gate_up.shape[2]
    step_heads = step_weight.shape[1]
    filter_rows, filter_columns = filter_state.shape
    small_width = 128

    small = jnp.concatenate(
        [
            step_weight,
            gain_in[:, None],
            gain_post[:, None],
            jnp.pad(filter_state, ((0, own_rows - filter_rows), (0, 0))),
        ],
        axis=1,
    )
    small = jnp.pad(small, ((0, 0), (0, small_width - small.shape[1])))
    first_pack = jnp.concatenate(
        [query_weight, shared_matrix, mixer_in.reshape(own_rows, 2 * channels), small], axis=1
    )
    second_pack = jnp.concatenate(
        [attention_out, mixer_out, gate_up.reshape(own_rows, 2 * hidden_units), down_weight], axis=1
    )
    seq_raw = gather_rows(inputs)
    first_all = lax.all_gather(first_pack, "dp", axis=0, tiled=True)
    first_all, second_pack, cotangent_sent = lax.optimization_barrier(
        (first_all, second_pack, cotangent)
    )
    second_all = lax.all_gather(second_pack, "dp", axis=0, tiled=True)
    back_seq = gather_rows(cotangent_sent)

    cut = query_width
    query_all = first_all[:, :cut]
    shared_all = first_all[:, cut : cut + shared_width]
    cut += shared_width
    mixer_in_all = first_all[:, cut : cut + 2 * channels]
    cut += 2 * channels
    small_all = first_all[:, cut:]
    step_all = small_all[:, :step_heads]
    gain_in_all = small_all[:, step_heads].astype(f32)
    gain_post_all = small_all[:, step_heads + 1].astype(f32)
    filter_state_all = (
        small_all[:, step_heads + 2 : step_heads + 2 + filter_columns]
        .reshape(dp_count, own_rows, filter_columns)[:, :filter_rows]
        .reshape(dp_count * filter_rows, filter_columns)
    )

    local_heads = query_width // HEAD_SIZE
    head_group = tensor_position * local_heads // (QUERY_HEADS // KEY_VALUE_HEADS)
    key_value_width = KEY_VALUE_HEADS * HEAD_SIZE
    channels_all = NH * PH
    filter_inner_f = filter_inner.astype(f32)
    step_bias_f = step_bias.astype(f32)
    log_decay_f = log_decay.astype(f32)
    skip_gain_f = skip_gain.astype(f32)
    mixer_gain_f = mixer_gain.astype(f32)
    inputs_f = inputs.astype(f32)
    scale_in = norm_scale(inputs_f)
    normed_in = inputs_f * scale_in
    seq_f = seq_raw.astype(f32)
    normed_seq = seq_f * norm_scale(seq_f)
    seq_in = (normed_seq * gain_in_all).astype(bf16)
    sequence_length = seq_in.shape[0]
    query = dot(seq_in, query_all)
    query_low = rotary_embed(
        query.reshape(sequence_length, local_heads, HEAD_SIZE), sequence_length, 1.0
    ).astype(bf16)
    key_cols = lax.dynamic_slice_in_dim(shared_all, head_group * HEAD_SIZE, HEAD_SIZE, 1)
    value_cols = lax.dynamic_slice_in_dim(
        shared_all, key_value_width + head_group * HEAD_SIZE, HEAD_SIZE, 1
    )
    used_cols = jnp.concatenate(
        [key_cols, value_cols, shared_all[:, 2 * key_value_width :]], axis=1
    )
    shared_projection = dot(seq_in, used_cols)
    keys_reduced = rotary_embed(shared_projection[:, None, :HEAD_SIZE], sequence_length, 1.0)[
        :, 0
    ].astype(bf16)
    values_reduced = shared_projection[:, HEAD_SIZE : 2 * HEAD_SIZE].astype(bf16)
    state_raw = shared_projection[:, 2 * HEAD_SIZE :]
    mixed, log_total = attend(query_low, keys_reduced, values_reduced, QB)
    mixed_low = mixed.astype(bf16)
    gate_z = dot(seq_in, mixer_in_all[:, :channels])
    inner_raw = dot(seq_in, mixer_in_all[:, channels:])
    step_raw = dot(seq_in, step_all)
    (inner, state_in, step_size), mixer_back = jax.vjp(
        mixer_input,
        inner_raw,
        state_raw,
        step_raw,
        filter_inner_f,
        filter_state_all.astype(f32),
        step_bias_f,
    )
    inner_low = inner.astype(bf16)
    state_low = state_in.astype(bf16)

    def scan_piece(inner_v, state_v, step_v, gate_v, decay_v, skip_v):
        return state_scan(inner_v, state_v, step_v, gate_v, decay_v, skip_v, BLK)

    gated, scan_back = jax.vjp(
        scan_piece,
        inner_low.astype(f32),
        state_low.astype(f32),
        step_size,
        gate_z,
        log_decay_f,
        skip_gain_f,
    )
    total_squares = lax.psum(jnp.sum(gated * gated, axis=1), "tensor")
    gated_scale = lax.rsqrt(total_squares / channels_all + epsilon)[:, None]
    gated_norm = gated * gated_scale
    mixer_low = (gated_norm * mixer_gain_f).astype(bf16)

    cut = query_width
    attention_all = second_all[:, :cut]
    mixer_out_all = second_all[:, cut : cut + channels]
    cut += channels
    gate_up_all = second_all[:, cut : cut + 2 * hidden_units]
    cut += 2 * hidden_units
    down_all = second_all[:, cut:]

    branch_low = (dot_t(mixed_low, attention_all) + dot_t(mixer_low, mixer_out_all)).astype(bf16)
    hidden = inputs_f + scatter_rows(branch_low)
    scale_post = norm_scale(hidden)
    normed_post = hidden * scale_post
    rows_post_low = (normed_post * gain_post_all).astype(bf16)
    seq_post = gather_rows(rows_post_low)
    gate = dot(seq_post, gate_up_all[:, :hidden_units])
    upper = dot(seq_post, gate_up_all[:, hidden_units:])
    sigmoid_gate = jax.nn.sigmoid(gate)
    silu_gate = gate * sigmoid_gate
    activated_low = (silu_gate * upper).astype(bf16)
    down_low = dot_t(activated_low, down_all).astype(bf16)

    back_act = dot(back_seq, down_all)
    back_gate = back_act * upper * sigmoid_gate * (1.0 + gate * (1.0 - sigmoid_gate))
    back_upper = back_act * silu_gate
    back_gu_low = jnp.concatenate([back_gate, back_upper], axis=1).astype(bf16)
    back_post_low = dot_t(back_gu_low, gate_up_all).astype(bf16)
    back_post = scatter_rows(back_post_low)
    back_down_w = t_dot(back_seq, activated_low).astype(bf16)
    back_gate_up_w = t_dot(seq_post, back_gu_low).astype(bf16)
    back_gain_post = jnp.sum(back_post * normed_post, axis=0)
    back_norm_post = back_post * gain_post_all
    back_hidden = cotangent.astype(f32) + scale_post * (
        back_norm_post - normed_post * jnp.mean(back_norm_post * normed_post, axis=1, keepdims=True)
    )
    back_mix = gather_rows(back_hidden.astype(bf16))
    output = (hidden + scatter_rows(down_low)).astype(bf16)

    back_mixer_out_w = t_dot(back_mix, mixer_low).astype(bf16)
    back_attention_w = t_dot(back_mix, mixed_low).astype(bf16)
    early = jnp.concatenate(
        [back_attention_w, back_mixer_out_w, back_gate_up_w, back_down_w], axis=1
    )
    early, back_mix = lax.optimization_barrier((early, back_mix))
    early_rows = lax.psum_scatter(early, "dp", scatter_dimension=0, tiled=True)

    back_norm = dot(back_mix, mixer_out_all)
    back_mixer_gain = jnp.sum(back_norm * gated_norm, axis=0)
    back_scaled = back_norm * mixer_gain_f
    inner_total = lax.psum(jnp.sum(back_scaled * gated_norm, axis=1), "tensor")
    back_gated = gated_scale * (back_scaled - gated_norm * (inner_total / channels_all)[:, None])
    back_inner, back_state, back_step_size, back_gate_z, back_log_decay, back_skip_gain = scan_back(
        back_gated
    )
    (
        back_inner_raw,
        back_state_raw,
        back_step_raw,
        back_filter_inner,
        back_filter_state,
        back_step_bias,
    ) = mixer_back((back_inner, back_state, back_step_size))
    back_mixer_low = jnp.concatenate([back_gate_z, back_inner_raw], axis=1).astype(bf16)
    back_step_low = back_step_raw.astype(bf16)
    back_mixed_low = dot(back_mix, attention_all).astype(bf16)
    back_query_rot, back_keys_rot, back_values = attend_back(
        query_low, keys_reduced, values_reduced, log_total, back_mixed_low, QB
    )
    back_query_low = (
        rotary_embed(back_query_rot, sequence_length, -1.0)
        .reshape(sequence_length, local_heads * HEAD_SIZE)
        .astype(bf16)
    )
    back_keys = rotary_embed(back_keys_rot[:, None, :], sequence_length, -1.0)[:, 0]
    back_used_low = jnp.concatenate([back_keys, back_values, back_state_raw], axis=1).astype(bf16)
    used_width = back_used_low.shape[1]

    back_in_part = (
        dot_t(back_query_low, query_all)
        + dot_t(back_mixer_low, mixer_in_all)
        + dot_t(back_step_low, step_all)
        + dot_t(back_used_low, used_cols)
    )
    back_gain_in = jnp.sum(back_in_part * normed_seq, axis=0)
    back_in_rows = scatter_rows(back_in_part.astype(bf16))

    spread_state = jnp.pad(
        back_filter_state.reshape(dp_count, filter_rows, filter_columns),
        ((0, 0), (0, own_rows - filter_rows), (0, 0)),
    ).reshape(width, filter_columns)
    back_small = jnp.concatenate(
        [
            t_dot(seq_in, back_step_low),
            back_gain_in[:, None],
            back_gain_post[:, None],
            spread_state,
        ],
        axis=1,
    )
    back_small = jnp.pad(back_small, ((0, 0), (0, small_width - back_small.shape[1])))
    late = jnp.concatenate(
        [
            t_dot(seq_in, back_query_low).astype(bf16),
            t_dot(seq_in, back_used_low).astype(bf16),
            t_dot(seq_in, back_mixer_low).astype(bf16),
            back_small.astype(bf16),
        ],
        axis=1,
    )
    late_rows = lax.psum_scatter(late, "dp", scatter_dimension=0, tiled=True)

    cut = query_width
    back_query_w = late_rows[:, :cut].astype(f32)
    used_rows = late_rows[:, cut : cut + used_width]
    cut += used_width
    back_mixer_in_w = late_rows[:, cut : cut + 2 * channels].astype(f32)
    cut += 2 * channels
    small_rows = late_rows[:, cut:]
    back_step_w = small_rows[:, :step_heads].astype(f32)
    select_heads = (jnp.arange(KEY_VALUE_HEADS) == head_group).astype(bf16)
    pair = (
        used_rows[:, : 2 * HEAD_SIZE].reshape(own_rows, 2, 1, HEAD_SIZE)
        * select_heads[None, None, :, None]
    ).reshape(own_rows, 2 * key_value_width)
    common = lax.psum(
        jnp.concatenate([pair, used_rows[:, 2 * HEAD_SIZE :], small_rows], axis=1), "tensor"
    ).astype(f32)
    back_shared_w = common[:, :shared_width]
    common = common[:, shared_width:]
    back_gain_in = common[:, step_heads]
    back_gain_post = common[:, step_heads + 1]
    back_filter_state = common[:filter_rows, step_heads + 2 : step_heads + 2 + filter_columns]

    cut = query_width
    back_attention_w = early_rows[:, :cut].astype(f32)
    back_mixer_out_w = early_rows[:, cut : cut + channels].astype(f32)
    cut += channels
    back_gate_up_w = early_rows[:, cut : cut + 2 * hidden_units].astype(f32)
    cut += 2 * hidden_units
    back_down_w = early_rows[:, cut:].astype(f32)

    back_norm_in = back_in_rows * gain_in_all
    back_inputs = back_hidden + scale_in * (
        back_norm_in - normed_in * jnp.mean(back_norm_in * normed_in, axis=1, keepdims=True)
    )
    pieces = (back_filter_inner, back_step_bias, back_log_decay, back_skip_gain, back_mixer_gain)
    flat = jnp.concatenate([piece.reshape(-1) for piece in pieces])
    flat = jnp.pad(flat, (0, -flat.shape[0] % 1024))
    flat = lax.psum(flat, "dp")
    results = []
    cut = 0
    for piece in pieces:
        results.append(flat[cut : cut + piece.size].reshape(piece.shape))
        cut += piece.size
    back_filter_inner, back_step_bias, back_log_decay, back_skip_gain, back_mixer_gain = results
    return (
        output,
        back_inputs,
        back_gain_in,
        back_query_w,
        back_shared_w,
        back_attention_w,
        back_mixer_in_w.reshape(own_rows, 2, channels),
        back_step_w,
        back_filter_inner,
        back_filter_state,
        back_step_bias,
        back_log_decay,
        back_skip_gain,
        back_mixer_gain,
        back_mixer_out_w,
        back_gain_post,
        back_gate_up_w.reshape(own_rows, 2, hidden_units),
        back_down_w,
    )


def solution(mesh):
    in_specs = (
        P(("dp", "tensor"), None),
        P(("dp", "tensor"), None),
        P("dp"),
        P("dp", "tensor"),
        P("dp", None),
        P("dp", "tensor"),
        P("dp", None, "tensor"),
        P("dp", "tensor"),
        P(None, "tensor"),
        P("dp", None),
        P("tensor"),
        P("tensor"),
        P("tensor"),
        P("tensor"),
        P("dp", "tensor"),
        P("dp"),
        P("dp", None, "tensor"),
        P("dp", "tensor"),
    )
    out_specs = (
        P(("dp", "tensor"), None),
        P(("dp", "tensor"), None),
        P("dp"),
        P("dp", "tensor"),
        P("dp", None),
        P("dp", "tensor"),
        P("dp", None, "tensor"),
        P("dp", "tensor"),
        P(None, "tensor"),
        P("dp", None),
        P("tensor"),
        P("tensor"),
        P("tensor"),
        P("tensor"),
        P("dp", "tensor"),
        P("dp"),
        P("dp", None, "tensor"),
        P("dp", "tensor"),
    )
    return jax.shard_map(body, mesh=mesh, in_specs=in_specs, out_specs=out_specs, check_vma=False)
```

```python
import jax
import jax.numpy as jnp
from jax import lax
from jax.sharding import PartitionSpec as P

QUERY_HEADS = 8
HEAD_SIZE = 64
KEY_VALUE_HEADS = 2
NH = 24
PH = 64
BLK = 128
QB = 512


epsilon = 1e-05
rope_base = 100000000000.0
highest_precision = lax.Precision.HIGHEST


def as_sent(x):

    def short(part):
        return part.astype(jnp.bfloat16) if part.dtype == jnp.float32 else part

    return jax.tree.map(short, x)


def norm_scale(values):
    return lax.rsqrt(jnp.mean(values * values, axis=-1, keepdims=True) + epsilon)


def rotary_embed(values, sequence_length, sign):
    half = values.shape[-1] // 2
    position = jnp.arange(sequence_length, dtype=jnp.float32)
    frequency = rope_base ** (-jnp.arange(half, dtype=jnp.float32) * 2.0 / values.shape[-1])
    angle = position[:, None] * frequency[None, :]
    cosine = jnp.cos(angle)[:, None, :]
    sine = sign * jnp.sin(angle)[:, None, :]
    first = values[..., :half]
    second = values[..., half:]
    return jnp.concatenate(
        [first * cosine - second * sine, second * cosine + first * sine], axis=-1
    )


def causal_filter(values, taps, bias):
    width = taps.shape[0]
    sequence_length = values.shape[0]
    padded = jnp.pad(values, ((width - 1, 0), (0, 0)))
    total = bias[None, :] + jnp.zeros_like(values)
    for offset in range(width):
        total = total + taps[offset][None, :] * padded[offset : offset + sequence_length]
    return total


def mixer_input(inner_raw, state_raw, step_raw, filter_inner, filter_state, step_bias):
    kernel = filter_inner.shape[0] - 1
    inner = jax.nn.silu(causal_filter(inner_raw, filter_inner[:kernel], filter_inner[kernel]))
    state_in = jax.nn.silu(
        causal_filter(state_raw, jnp.transpose(filter_state[:, :kernel]), filter_state[:, kernel])
    )
    step_size = jax.nn.softplus(step_raw + step_bias[None, :])
    return (inner, state_in, step_size)


def state_scan(inner, state_in, step_size, gate_z, log_decay, skip_gain, block):
    sequence_length, channels = inner.shape
    heads = step_size.shape[1]
    head = channels // heads
    state_width = state_in.shape[1] // 2
    count = sequence_length // block
    inner_blocks = inner.reshape(count, block, heads, head)
    state_input_keys = state_in[:, :state_width].reshape(count, block, state_width)
    state_output_reads = state_in[:, state_width:].reshape(count, block, state_width)
    rate = step_size * (-jnp.exp(log_decay))[None, :]
    running = jnp.cumsum(rate.reshape(count, block, heads), axis=1)
    step_blocks = step_size.reshape(count, block, heads)
    within_group = jnp.einsum(
        "xfw,xkw->xfk", state_output_reads, state_input_keys, precision=highest_precision
    )
    lower = jnp.arange(block)[:, None] >= jnp.arange(block)[None, :]
    spread = running[:, :, None, :] - running[:, None, :, :]
    decay = jnp.exp(jnp.where(lower[None, :, :, None], spread, -1e30))
    mixing = within_group[..., None] * decay * step_blocks[:, None, :, :]
    local_out = jnp.einsum("clrh,crhp->clhp", mixing, inner_blocks, precision=highest_precision)
    tail = jnp.exp(running[:, -1:, :] - running) * step_blocks
    block_state = jnp.einsum(
        "crh,crhp,crn->chpn", tail, inner_blocks, state_input_keys, precision=highest_precision
    )
    total_decay = jnp.exp(running[:, -1, :])

    carry = jnp.zeros((heads, head, state_width), inner.dtype)
    states = []
    for index in range(count):
        states.append(carry)
        carry = carry * total_decay[index][:, None, None] + block_state[index]
    entering = jnp.stack(states)
    carried = (
        jnp.einsum("cln,chpn->clhp", state_output_reads, entering, precision=highest_precision)
        * jnp.exp(running)[..., None]
    )
    result = (local_out + carried).reshape(sequence_length, channels) + inner * jnp.repeat(
        skip_gain, head
    )[None, :]
    return result * jax.nn.silu(gate_z)


def attend(query_low, keys_reduced, values_reduced, block):
    sequence_length, heads, head = query_low.shape
    scale = head ** (-0.5)
    parts = []
    totals = []
    for start in range(0, sequence_length, block):
        end = start + block
        rows = query_low[start:end]
        scores = (
            jnp.einsum("qhd,kd->hqk", rows, keys_reduced[:end], preferred_element_type=jnp.float32)
            * scale
        )
        visible = (start + jnp.arange(block))[:, None] >= jnp.arange(end)[None, :]
        scores = jnp.where(visible[None], scores, -1e30)
        peak = jnp.max(scores, axis=-1, keepdims=True)
        weights = jnp.exp(scores - peak)
        total = jnp.sum(weights, axis=-1, keepdims=True)
        shares_low = (weights / total).astype(jnp.bfloat16)
        parts.append(
            jnp.einsum(
                "hqk,kd->qhd", shares_low, values_reduced[:end], preferred_element_type=jnp.float32
            ).reshape(block, heads * head)
        )
        totals.append(peak + jnp.log(total))
    return (jnp.concatenate(parts, axis=0), totals)


def attend_back(query_low, keys_reduced, values_reduced, totals, back_mixed_low, block):
    sequence_length, heads, head = query_low.shape
    scale = head ** (-0.5)
    back_view = back_mixed_low.reshape(sequence_length, heads, head)
    back_keys = jnp.zeros((sequence_length, head), jnp.float32)
    back_values = jnp.zeros((sequence_length, head), jnp.float32)
    queries = []
    for index, start in enumerate(range(0, sequence_length, block)):
        end = start + block
        rows = query_low[start:end]
        back_rows = back_view[start:end]
        scores = (
            jnp.einsum("qhd,kd->hqk", rows, keys_reduced[:end], preferred_element_type=jnp.float32)
            * scale
        )
        visible = (start + jnp.arange(block))[:, None] >= jnp.arange(end)[None, :]
        shares = jnp.where(visible[None], jnp.exp(jnp.where(visible[None], scores - totals[index], -1e30)), 0.0)
        back_shares = jnp.einsum(
            "qhd,kd->hqk", back_rows, values_reduced[:end], preferred_element_type=jnp.float32
        )
        inner = jnp.sum(shares * back_shares, axis=-1, keepdims=True)
        back_scores = (shares * (back_shares - inner)).astype(jnp.bfloat16)
        queries.append(
            jnp.einsum(
                "hqk,kd->qhd", back_scores, keys_reduced[:end], preferred_element_type=jnp.float32
            )
            * scale
        )
        rest = ((0, sequence_length - end), (0, 0))
        back_keys = back_keys + jnp.pad(
            jnp.einsum("hqk,qhd->kd", back_scores, rows, preferred_element_type=jnp.float32)
            * scale,
            rest,
        )
        back_values = back_values + jnp.pad(
            jnp.einsum(
                "hqk,qhd->kd",
                shares.astype(jnp.bfloat16),
                back_rows,
                preferred_element_type=jnp.float32,
            ),
            rest,
        )
    return (jnp.concatenate(queries, axis=0), back_keys, back_values)


def swap(values, axis, count, bit):
    return lax.ppermute(values, axis, [(i, i ^ bit) for i in range(count)])


def gather_rows(values):
    count = lax.axis_size("tensor")
    if count & (count - 1):
        return lax.all_gather(values, "tensor", axis=0, tiled=True)
    index = lax.axis_index("tensor")
    rows, width = values.shape
    held = values[None]
    bit = count // 2
    while bit:
        other = swap(held, "tensor", count, bit)
        low = (index // bit) % 2 == 0
        held = jnp.stack([jnp.where(low, held, other), jnp.where(low, other, held)], axis=1)
        held = held.reshape(-1, rows, width)
        bit //= 2
    return held.reshape(count * rows, width)


def scatter_rows(values):
    count = lax.axis_size("tensor")
    if count & (count - 1):
        return lax.psum_scatter(values, "tensor", scatter_dimension=0, tiled=True).astype(
            jnp.float32
        )
    index = lax.axis_index("tensor")
    rows = values.shape[0] // count
    width = values.shape[1]
    total = values.reshape(count, rows, width)
    bit = 1
    while bit < count:
        pairs = total.reshape(-1, 2, rows, width)
        mine = (index // bit) % 2
        kept = lax.dynamic_index_in_dim(pairs, mine, 1, keepdims=False)
        sent = lax.dynamic_index_in_dim(pairs, 1 - mine, 1, keepdims=False).astype(jnp.bfloat16)
        total = kept.astype(jnp.float32) + swap(sent, "tensor", count, bit).astype(jnp.float32)
        bit *= 2
    return total.reshape(rows, width)


def sum_all(values, axis):
    count = lax.axis_size(axis)
    if count & (count - 1):
        return lax.psum(values, axis)
    bit = 1
    while bit < count:
        values = values + swap(values, axis, count, bit)
        bit *= 2
    return values


def body(
    inputs,
    cotangent,
    gain_in,
    query_weight,
    shared_matrix,
    attention_out,
    mixer_in,
    step_weight,
    filter_inner,
    filter_state,
    step_bias,
    log_decay,
    skip_gain,
    mixer_gain,
    mixer_out,
    gain_post,
    gate_up,
    down_weight,
):
    tensor_position = lax.axis_index("tensor")
    bf16 = jnp.bfloat16
    f32 = jnp.float32

    def dot(left, right):
        return jnp.dot(left, right, preferred_element_type=f32)

    def dot_t(left, right):
        return lax.dot_general(left, right, (((1,), (1,)), ((), ())), preferred_element_type=f32)

    def t_dot(left, right):
        return lax.dot_general(left, right, (((0,), (0,)), ((), ())), preferred_element_type=f32)

    own_rows = query_weight.shape[0]
    width = inputs.shape[1]
    dp_count = width // own_rows
    query_width = query_weight.shape[1]
    shared_width = shared_matrix.shape[1]
    channels = mixer_in.shape[2]
    hidden_units = gate_up.shape[2]
    step_heads = step_weight.shape[1]
    filter_rows, filter_columns = filter_state.shape
    small_width = 128

    small = jnp.concatenate(
        [
            step_weight,
            gain_in[:, None],
            gain_post[:, None],
            jnp.pad(filter_state, ((0, own_rows - filter_rows), (0, 0))),
        ],
        axis=1,
    )
    small = jnp.pad(small, ((0, 0), (0, small_width - small.shape[1])))
    first_pack = jnp.concatenate(
        [query_weight, shared_matrix, mixer_in.reshape(own_rows, 2 * channels), small], axis=1
    )
    second_pack = jnp.concatenate(
        [attention_out, mixer_out, gate_up.reshape(own_rows, 2 * hidden_units), down_weight], axis=1
    )
    seq_raw = gather_rows(inputs)
    first_all = lax.all_gather(first_pack, "dp", axis=0, tiled=True)
    first_all, second_pack, cotangent_sent = lax.optimization_barrier(
        (first_all, second_pack, cotangent)
    )
    second_all = lax.all_gather(second_pack, "dp", axis=0, tiled=True)
    back_seq = gather_rows(cotangent_sent)

    cut = query_width
    query_all = first_all[:, :cut]
    shared_all = first_all[:, cut : cut + shared_width]
    cut += shared_width
    mixer_in_all = first_all[:, cut : cut + 2 * channels]
    cut += 2 * channels
    small_all = first_all[:, cut:]
    step_all = small_all[:, :step_heads]
    gain_in_all = small_all[:, step_heads].astype(f32)
    gain_post_all = small_all[:, step_heads + 1].astype(f32)
    filter_state_all = (
        small_all[:, step_heads + 2 : step_heads + 2 + filter_columns]
        .reshape(dp_count, own_rows, filter_columns)[:, :filter_rows]
        .reshape(dp_count * filter_rows, filter_columns)
    )

    local_heads = query_width // HEAD_SIZE
    head_group = tensor_position * local_heads // (QUERY_HEADS // KEY_VALUE_HEADS)
    key_value_width = KEY_VALUE_HEADS * HEAD_SIZE
    channels_all = NH * PH
    filter_inner_f = filter_inner.astype(f32)
    step_bias_f = step_bias.astype(f32)
    log_decay_f = log_decay.astype(f32)
    skip_gain_f = skip_gain.astype(f32)
    mixer_gain_f = mixer_gain.astype(f32)
    inputs_f = inputs.astype(f32)
    scale_in = norm_scale(inputs_f)
    normed_in = inputs_f * scale_in
    seq_f = seq_raw.astype(f32)
    normed_seq = seq_f * norm_scale(seq_f)
    seq_in = (normed_seq * gain_in_all).astype(bf16)
    sequence_length = seq_in.shape[0]
    query = dot(seq_in, query_all)
    query_low = rotary_embed(
        query.reshape(sequence_length, local_heads, HEAD_SIZE), sequence_length, 1.0
    ).astype(bf16)
    key_cols = lax.dynamic_slice_in_dim(shared_all, head_group * HEAD_SIZE, HEAD_SIZE, 1)
    value_cols = lax.dynamic_slice_in_dim(
        shared_all, key_value_width + head_group * HEAD_SIZE, HEAD_SIZE, 1
    )
    used_cols = jnp.concatenate(
        [key_cols, value_cols, shared_all[:, 2 * key_value_width :]], axis=1
    )
    shared_projection = dot(seq_in, used_cols)
    keys_reduced = rotary_embed(shared_projection[:, None, :HEAD_SIZE], sequence_length, 1.0)[
        :, 0
    ].astype(bf16)
    values_reduced = shared_projection[:, HEAD_SIZE : 2 * HEAD_SIZE].astype(bf16)
    state_raw = shared_projection[:, 2 * HEAD_SIZE :]
    mixed, log_total = attend(query_low, keys_reduced, values_reduced, QB)
    mixed_low = mixed.astype(bf16)
    gate_z = dot(seq_in, mixer_in_all[:, :channels])
    inner_raw = dot(seq_in, mixer_in_all[:, channels:])
    step_raw = dot(seq_in, step_all)
    (inner, state_in, step_size), mixer_back = jax.vjp(
        mixer_input,
        inner_raw,
        state_raw,
        step_raw,
        filter_inner_f,
        filter_state_all.astype(f32),
        step_bias_f,
    )
    inner_low = inner.astype(bf16)
    state_low = state_in.astype(bf16)

    def scan_piece(inner_v, state_v, step_v, gate_v, decay_v, skip_v):
        return state_scan(inner_v, state_v, step_v, gate_v, decay_v, skip_v, BLK)

    gated, scan_back = jax.vjp(
        scan_piece,
        inner_low.astype(f32),
        state_low.astype(f32),
        step_size,
        gate_z,
        log_decay_f,
        skip_gain_f,
    )
    total_squares = lax.psum(jnp.sum(gated * gated, axis=1), "tensor")
    gated_scale = lax.rsqrt(total_squares / channels_all + epsilon)[:, None]
    gated_norm = gated * gated_scale
    mixer_low = (gated_norm * mixer_gain_f).astype(bf16)

    cut = query_width
    attention_all = second_all[:, :cut]
    mixer_out_all = second_all[:, cut : cut + channels]
    cut += channels
    gate_up_all = second_all[:, cut : cut + 2 * hidden_units]
    cut += 2 * hidden_units
    down_all = second_all[:, cut:]

    mixer_low, back_seq = lax.optimization_barrier((mixer_low, back_seq))
    branch_low = (dot_t(mixed_low, attention_all) + dot_t(mixer_low, mixer_out_all)).astype(bf16)
    hidden = inputs_f + scatter_rows(branch_low)
    scale_post = norm_scale(hidden)
    normed_post = hidden * scale_post
    rows_post_low = (normed_post * gain_post_all).astype(bf16)
    seq_post = gather_rows(rows_post_low)
    gate = dot(seq_post, gate_up_all[:, :hidden_units])
    upper = dot(seq_post, gate_up_all[:, hidden_units:])
    sigmoid_gate = jax.nn.sigmoid(gate)
    silu_gate = gate * sigmoid_gate
    activated_low = (silu_gate * upper).astype(bf16)
    down_low = dot_t(activated_low, down_all).astype(bf16)

    back_act = dot(back_seq, down_all)
    back_gate = back_act * upper * sigmoid_gate * (1.0 + gate * (1.0 - sigmoid_gate))
    back_upper = back_act * silu_gate
    back_gu_low = jnp.concatenate([back_gate, back_upper], axis=1).astype(bf16)
    back_post_low = dot_t(back_gu_low, gate_up_all).astype(bf16)
    back_post = scatter_rows(back_post_low)
    back_down_w = t_dot(back_seq, activated_low).astype(bf16)
    back_gate_up_w = t_dot(seq_post, back_gu_low).astype(bf16)
    back_gain_post = jnp.sum(back_post * normed_post, axis=0)
    back_norm_post = back_post * gain_post_all
    back_hidden = cotangent.astype(f32) + scale_post * (
        back_norm_post - normed_post * jnp.mean(back_norm_post * normed_post, axis=1, keepdims=True)
    )
    back_mix = gather_rows(back_hidden.astype(bf16))

    back_mixer_out_w = t_dot(back_mix, mixer_low).astype(bf16)
    back_attention_w = t_dot(back_mix, mixed_low).astype(bf16)
    early = jnp.concatenate(
        [back_attention_w, back_mixer_out_w, back_gate_up_w, back_down_w], axis=1
    )
    early, back_mix, down_low = lax.optimization_barrier((early, back_mix, down_low))
    down_rows = scatter_rows(down_low)
    early_rows = lax.psum_scatter(early, "dp", scatter_dimension=0, tiled=True)

    back_norm = dot(back_mix, mixer_out_all)
    back_mixer_gain = jnp.sum(back_norm * gated_norm, axis=0)
    back_scaled = back_norm * mixer_gain_f
    inner_total = lax.psum(jnp.sum(back_scaled * gated_norm, axis=1), "tensor")
    back_gated = gated_scale * (back_scaled - gated_norm * (inner_total / channels_all)[:, None])
    back_inner, back_state, back_step_size, back_gate_z, back_log_decay, back_skip_gain = scan_back(
        back_gated
    )
    (
        back_inner_raw,
        back_state_raw,
        back_step_raw,
        back_filter_inner,
        back_filter_state,
        back_step_bias,
    ) = mixer_back((back_inner, back_state, back_step_size))
    back_mixer_low = jnp.concatenate([back_gate_z, back_inner_raw], axis=1).astype(bf16)
    back_step_low = back_step_raw.astype(bf16)
    back_mixed_low = dot(back_mix, attention_all).astype(bf16)
    back_query_rot, back_keys_rot, back_values = attend_back(
        query_low, keys_reduced, values_reduced, log_total, back_mixed_low, QB
    )
    back_query_low = (
        rotary_embed(back_query_rot, sequence_length, -1.0)
        .reshape(sequence_length, local_heads * HEAD_SIZE)
        .astype(bf16)
    )
    back_keys = rotary_embed(back_keys_rot[:, None, :], sequence_length, -1.0)[:, 0]
    back_used_low = jnp.concatenate([back_keys, back_values, back_state_raw], axis=1).astype(bf16)
    used_width = back_used_low.shape[1]

    back_mixer_low, back_query_low, back_used_low, early_rows, down_rows = lax.optimization_barrier(
        (back_mixer_low, back_query_low, back_used_low, early_rows, down_rows)
    )
    output = (hidden + down_rows).astype(bf16)
    back_in_part = (
        dot_t(back_query_low, query_all)
        + dot_t(back_mixer_low, mixer_in_all)
        + dot_t(back_step_low, step_all)
        + dot_t(back_used_low, used_cols)
    )
    back_gain_in = jnp.sum(back_in_part * normed_seq, axis=0)
    back_in_rows = scatter_rows(back_in_part.astype(bf16))

    spread_state = jnp.pad(
        back_filter_state.reshape(dp_count, filter_rows, filter_columns),
        ((0, 0), (0, own_rows - filter_rows), (0, 0)),
    ).reshape(width, filter_columns)
    back_small = jnp.concatenate(
        [
            t_dot(seq_in, back_step_low),
            back_gain_in[:, None],
            back_gain_post[:, None],
            spread_state,
        ],
        axis=1,
    )
    back_small = jnp.pad(back_small, ((0, 0), (0, small_width - back_small.shape[1])))
    late = jnp.concatenate(
        [
            t_dot(seq_in, back_query_low).astype(bf16),
            t_dot(seq_in, back_used_low).astype(bf16),
            t_dot(seq_in, back_mixer_low).astype(bf16),
            back_small.astype(bf16),
        ],
        axis=1,
    )
    late_rows = lax.psum_scatter(late, "dp", scatter_dimension=0, tiled=True)

    cut = query_width
    back_query_w = late_rows[:, :cut].astype(f32)
    used_rows = late_rows[:, cut : cut + used_width]
    cut += used_width
    back_mixer_in_w = late_rows[:, cut : cut + 2 * channels].astype(f32)
    cut += 2 * channels
    small_rows = late_rows[:, cut:]
    back_step_w = small_rows[:, :step_heads].astype(f32)
    select_heads = (jnp.arange(KEY_VALUE_HEADS) == head_group).astype(bf16)
    pair = (
        used_rows[:, : 2 * HEAD_SIZE].reshape(own_rows, 2, 1, HEAD_SIZE)
        * select_heads[None, None, :, None]
    ).reshape(own_rows, 2 * key_value_width)
    common = sum_all(
        jnp.concatenate([pair, used_rows[:, 2 * HEAD_SIZE :], small_rows], axis=1), "tensor"
    ).astype(f32)
    back_shared_w = common[:, :shared_width]
    common = common[:, shared_width:]
    back_gain_in = common[:, step_heads]
    back_gain_post = common[:, step_heads + 1]
    back_filter_state = common[:filter_rows, step_heads + 2 : step_heads + 2 + filter_columns]

    cut = query_width
    back_attention_w = early_rows[:, :cut].astype(f32)
    back_mixer_out_w = early_rows[:, cut : cut + channels].astype(f32)
    cut += channels
    back_gate_up_w = early_rows[:, cut : cut + 2 * hidden_units].astype(f32)
    cut += 2 * hidden_units
    back_down_w = early_rows[:, cut:].astype(f32)

    back_norm_in = back_in_rows * gain_in_all
    back_inputs = back_hidden + scale_in * (
        back_norm_in - normed_in * jnp.mean(back_norm_in * normed_in, axis=1, keepdims=True)
    )
    pieces = (back_filter_inner, back_step_bias, back_log_decay, back_skip_gain, back_mixer_gain)
    flat = jnp.concatenate([piece.reshape(-1) for piece in pieces])
    flat = jnp.pad(flat, (0, -flat.shape[0] % 1024))
    flat = sum_all(flat, "dp")
    results = []
    cut = 0
    for piece in pieces:
        results.append(flat[cut : cut + piece.size].reshape(piece.shape))
        cut += piece.size
    back_filter_inner, back_step_bias, back_log_decay, back_skip_gain, back_mixer_gain = results
    return (
        output,
        back_inputs,
        back_gain_in,
        back_query_w,
        back_shared_w,
        back_attention_w,
        back_mixer_in_w.reshape(own_rows, 2, channels),
        back_step_w,
        back_filter_inner,
        back_filter_state,
        back_step_bias,
        back_log_decay,
        back_skip_gain,
        back_mixer_gain,
        back_mixer_out_w,
        back_gain_post,
        back_gate_up_w.reshape(own_rows, 2, hidden_units),
        back_down_w,
    )


def solution(mesh):
    in_specs = (
        P(("dp", "tensor"), None),
        P(("dp", "tensor"), None),
        P("dp"),
        P("dp", "tensor"),
        P("dp", None),
        P("dp", "tensor"),
        P("dp", None, "tensor"),
        P("dp", "tensor"),
        P(None, "tensor"),
        P("dp", None),
        P("tensor"),
        P("tensor"),
        P("tensor"),
        P("tensor"),
        P("dp", "tensor"),
        P("dp"),
        P("dp", None, "tensor"),
        P("dp", "tensor"),
    )
    out_specs = (
        P(("dp", "tensor"), None),
        P(("dp", "tensor"), None),
        P("dp"),
        P("dp", "tensor"),
        P("dp", None),
        P("dp", "tensor"),
        P("dp", None, "tensor"),
        P("dp", "tensor"),
        P(None, "tensor"),
        P("dp", None),
        P("tensor"),
        P("tensor"),
        P("tensor"),
        P("tensor"),
        P("dp", "tensor"),
        P("dp"),
        P("dp", None, "tensor"),
        P("dp", "tensor"),
    )
    return jax.shard_map(body, mesh=mesh, in_specs=in_specs, out_specs=out_specs, check_vma=False)
```

```python
import jax
import jax.numpy as jnp
from jax import lax
from jax.sharding import PartitionSpec as P

QUERY_HEADS = 8
HEAD_SIZE = 64
KEY_VALUE_HEADS = 2
NH = 24
PH = 64
BLK = 128
QB = 512


epsilon = 1e-05
rope_base = 100000000000.0
highest_precision = lax.Precision.HIGHEST


def as_sent(x):

    def short(part):
        return part.astype(jnp.bfloat16) if part.dtype == jnp.float32 else part

    return jax.tree.map(short, x)


def norm_scale(values):
    return lax.rsqrt(jnp.mean(values * values, axis=-1, keepdims=True) + epsilon)


def rotary_embed(values, sequence_length, sign):
    half = values.shape[-1] // 2
    position = jnp.arange(sequence_length, dtype=jnp.float32)
    frequency = rope_base ** (-jnp.arange(half, dtype=jnp.float32) * 2.0 / values.shape[-1])
    angle = position[:, None] * frequency[None, :]
    cosine = jnp.cos(angle)[:, None, :]
    sine = sign * jnp.sin(angle)[:, None, :]
    first = values[..., :half]
    second = values[..., half:]
    return jnp.concatenate(
        [first * cosine - second * sine, second * cosine + first * sine], axis=-1
    )


def causal_filter(values, taps, bias):
    width = taps.shape[0]
    sequence_length = values.shape[0]
    padded = jnp.pad(values, ((width - 1, 0), (0, 0)))
    total = bias[None, :] + jnp.zeros_like(values)
    for offset in range(width):
        total = total + taps[offset][None, :] * padded[offset : offset + sequence_length]
    return total


def mixer_input(inner_raw, state_raw, step_raw, filter_inner, filter_state, step_bias):
    kernel = filter_inner.shape[0] - 1
    inner = jax.nn.silu(causal_filter(inner_raw, filter_inner[:kernel], filter_inner[kernel]))
    state_in = jax.nn.silu(
        causal_filter(state_raw, jnp.transpose(filter_state[:, :kernel]), filter_state[:, kernel])
    )
    step_size = jax.nn.softplus(step_raw + step_bias[None, :])
    return (inner, state_in, step_size)


def state_scan(inner, state_in, step_size, gate_z, log_decay, skip_gain, block):
    sequence_length, channels = inner.shape
    heads = step_size.shape[1]
    head = channels // heads
    state_width = state_in.shape[1] // 2
    count = sequence_length // block
    inner_blocks = inner.reshape(count, block, heads, head)
    state_input_keys = state_in[:, :state_width].reshape(count, block, state_width)
    state_output_reads = state_in[:, state_width:].reshape(count, block, state_width)
    rate = step_size * (-jnp.exp(log_decay))[None, :]
    running = jnp.cumsum(rate.reshape(count, block, heads), axis=1)
    step_blocks = step_size.reshape(count, block, heads)
    within_group = jnp.einsum(
        "xfw,xkw->xfk", state_output_reads, state_input_keys, precision=highest_precision
    )
    lower = jnp.arange(block)[:, None] >= jnp.arange(block)[None, :]
    spread = running[:, :, None, :] - running[:, None, :, :]
    decay = jnp.exp(jnp.where(lower[None, :, :, None], spread, -1e30))
    mixing = within_group[..., None] * decay * step_blocks[:, None, :, :]
    local_out = jnp.einsum("clrh,crhp->clhp", mixing, inner_blocks, precision=highest_precision)
    tail = jnp.exp(running[:, -1:, :] - running) * step_blocks
    block_state = jnp.einsum(
        "crh,crhp,crn->chpn", tail, inner_blocks, state_input_keys, precision=highest_precision
    )
    total_decay = jnp.exp(running[:, -1, :])

    carry = jnp.zeros((heads, head, state_width), inner.dtype)
    states = []
    for index in range(count):
        states.append(carry)
        carry = carry * total_decay[index][:, None, None] + block_state[index]
    entering = jnp.stack(states)
    carried = (
        jnp.einsum("cln,chpn->clhp", state_output_reads, entering, precision=highest_precision)
        * jnp.exp(running)[..., None]
    )
    result = (local_out + carried).reshape(sequence_length, channels) + inner * jnp.repeat(
        skip_gain, head
    )[None, :]
    return result * jax.nn.silu(gate_z)


def attend(query_low, keys_reduced, values_reduced, block):
    sequence_length, heads, head = query_low.shape
    scale = head ** (-0.5)
    parts = []
    totals = []
    for start in range(0, sequence_length, block):
        end = start + block
        rows = query_low[start:end]
        scores = (
            jnp.einsum("qhd,kd->hqk", rows, keys_reduced[:end], preferred_element_type=jnp.float32)
            * scale
        )
        visible = (start + jnp.arange(block))[:, None] >= jnp.arange(end)[None, :]
        scores = jnp.where(visible[None], scores, -1e30)
        peak = jnp.max(scores, axis=-1, keepdims=True)
        weights = jnp.exp(scores - peak)
        total = jnp.sum(weights, axis=-1, keepdims=True)
        shares_low = (weights / total).astype(jnp.bfloat16)
        parts.append(
            jnp.einsum(
                "hqk,kd->qhd", shares_low, values_reduced[:end], preferred_element_type=jnp.float32
            ).reshape(block, heads * head)
        )
        totals.append(peak + jnp.log(total))
    return (jnp.concatenate(parts, axis=0), totals)


def attend_back(query_low, keys_reduced, values_reduced, totals, back_mixed_low, block):
    sequence_length, heads, head = query_low.shape
    scale = head ** (-0.5)
    back_view = back_mixed_low.reshape(sequence_length, heads, head)
    back_keys = jnp.zeros((sequence_length, head), jnp.float32)
    back_values = jnp.zeros((sequence_length, head), jnp.float32)
    queries = []
    for index, start in enumerate(range(0, sequence_length, block)):
        end = start + block
        rows = query_low[start:end]
        back_rows = back_view[start:end]
        scores = (
            jnp.einsum("qhd,kd->hqk", rows, keys_reduced[:end], preferred_element_type=jnp.float32)
            * scale
        )
        visible = (start + jnp.arange(block))[:, None] >= jnp.arange(end)[None, :]
        shares = jnp.where(visible[None], jnp.exp(jnp.where(visible[None], scores - totals[index], -1e30)), 0.0)
        back_shares = jnp.einsum(
            "qhd,kd->hqk", back_rows, values_reduced[:end], preferred_element_type=jnp.float32
        )
        inner = jnp.sum(shares * back_shares, axis=-1, keepdims=True)
        back_scores = (shares * (back_shares - inner)).astype(jnp.bfloat16)
        queries.append(
            jnp.einsum(
                "hqk,kd->qhd", back_scores, keys_reduced[:end], preferred_element_type=jnp.float32
            )
            * scale
        )
        rest = ((0, sequence_length - end), (0, 0))
        back_keys = back_keys + jnp.pad(
            jnp.einsum("hqk,qhd->kd", back_scores, rows, preferred_element_type=jnp.float32)
            * scale,
            rest,
        )
        back_values = back_values + jnp.pad(
            jnp.einsum(
                "hqk,qhd->kd",
                shares.astype(jnp.bfloat16),
                back_rows,
                preferred_element_type=jnp.float32,
            ),
            rest,
        )
    return (jnp.concatenate(queries, axis=0), back_keys, back_values)


def swap(values, axis, count, bit):
    return lax.ppermute(values, axis, [(i, i ^ bit) for i in range(count)])


def gather_rows(values):
    count = lax.axis_size("tensor")
    if count & (count - 1):
        return lax.all_gather(values, "tensor", axis=0, tiled=True)
    index = lax.axis_index("tensor")
    rows, width = values.shape
    held = values[None]
    bit = count // 2
    while bit:
        other = swap(held, "tensor", count, bit)
        low = (index // bit) % 2 == 0
        held = jnp.stack([jnp.where(low, held, other), jnp.where(low, other, held)], axis=1)
        held = held.reshape(-1, rows, width)
        bit //= 2
    return held.reshape(count * rows, width)


def scatter_bits(total, axis, bits):
    count = lax.axis_size(axis)
    index = lax.axis_index(axis)
    rows, width = total.shape[1:]
    for bit in bits:
        pairs = total.reshape(-1, 2, rows, width)
        mine = (index // bit) % 2
        kept = lax.dynamic_index_in_dim(pairs, mine, 1, keepdims=False)
        sent = lax.dynamic_index_in_dim(pairs, 1 - mine, 1, keepdims=False).astype(jnp.bfloat16)
        total = kept.astype(jnp.float32) + swap(sent, axis, count, bit).astype(jnp.float32)
    return total


def scatter_rows(values, axis="tensor"):
    count = lax.axis_size(axis)
    if count & (count - 1):
        return lax.psum_scatter(values, axis, scatter_dimension=0, tiled=True).astype(jnp.float32)
    rows = values.shape[0] // count
    width = values.shape[1]
    bits = [1 << k for k in range(count.bit_length() - 1)]
    return scatter_bits(values.reshape(count, rows, width), axis, bits).reshape(rows, width)


def sum_all(values, axis):
    count = lax.axis_size(axis)
    if count & (count - 1):
        return lax.psum(values, axis)
    bit = 1
    while bit < count:
        values = values + swap(values, axis, count, bit)
        bit *= 2
    return values


def body(
    inputs,
    cotangent,
    gain_in,
    query_weight,
    shared_matrix,
    attention_out,
    mixer_in,
    step_weight,
    filter_inner,
    filter_state,
    step_bias,
    log_decay,
    skip_gain,
    mixer_gain,
    mixer_out,
    gain_post,
    gate_up,
    down_weight,
):
    tensor_position = lax.axis_index("tensor")
    bf16 = jnp.bfloat16
    f32 = jnp.float32

    def dot(left, right):
        return jnp.dot(left, right, preferred_element_type=f32)

    def dot_t(left, right):
        return lax.dot_general(left, right, (((1,), (1,)), ((), ())), preferred_element_type=f32)

    def t_dot(left, right):
        return lax.dot_general(left, right, (((0,), (0,)), ((), ())), preferred_element_type=f32)

    own_rows = query_weight.shape[0]
    width = inputs.shape[1]
    dp_count = width // own_rows
    query_width = query_weight.shape[1]
    shared_width = shared_matrix.shape[1]
    channels = mixer_in.shape[2]
    hidden_units = gate_up.shape[2]
    step_heads = step_weight.shape[1]
    filter_rows, filter_columns = filter_state.shape
    small_width = 128

    small = jnp.concatenate(
        [
            step_weight,
            gain_in[:, None],
            gain_post[:, None],
            jnp.pad(filter_state, ((0, own_rows - filter_rows), (0, 0))),
        ],
        axis=1,
    )
    small = jnp.pad(small, ((0, 0), (0, small_width - small.shape[1])))
    first_pack = jnp.concatenate(
        [query_weight, shared_matrix, mixer_in.reshape(own_rows, 2 * channels), small], axis=1
    )
    second_pack = jnp.concatenate(
        [attention_out, mixer_out, gate_up.reshape(own_rows, 2 * hidden_units), down_weight], axis=1
    )
    seq_raw = gather_rows(inputs)
    first_all = lax.all_gather(first_pack, "dp", axis=0, tiled=True)
    first_all, second_pack, cotangent_sent = lax.optimization_barrier(
        (first_all, second_pack, cotangent)
    )
    second_all = lax.all_gather(second_pack, "dp", axis=0, tiled=True)
    back_seq = gather_rows(cotangent_sent)

    cut = query_width
    query_all = first_all[:, :cut]
    shared_all = first_all[:, cut : cut + shared_width]
    cut += shared_width
    mixer_in_all = first_all[:, cut : cut + 2 * channels]
    cut += 2 * channels
    small_all = first_all[:, cut:]
    step_all = small_all[:, :step_heads]
    gain_in_all = small_all[:, step_heads].astype(f32)
    gain_post_all = small_all[:, step_heads + 1].astype(f32)
    filter_state_all = (
        small_all[:, step_heads + 2 : step_heads + 2 + filter_columns]
        .reshape(dp_count, own_rows, filter_columns)[:, :filter_rows]
        .reshape(dp_count * filter_rows, filter_columns)
    )

    local_heads = query_width // HEAD_SIZE
    head_group = tensor_position * local_heads // (QUERY_HEADS // KEY_VALUE_HEADS)
    key_value_width = KEY_VALUE_HEADS * HEAD_SIZE
    channels_all = NH * PH
    filter_inner_f = filter_inner.astype(f32)
    step_bias_f = step_bias.astype(f32)
    log_decay_f = log_decay.astype(f32)
    skip_gain_f = skip_gain.astype(f32)
    mixer_gain_f = mixer_gain.astype(f32)
    inputs_f = inputs.astype(f32)
    scale_in = norm_scale(inputs_f)
    normed_in = inputs_f * scale_in
    seq_f = seq_raw.astype(f32)
    normed_seq = seq_f * norm_scale(seq_f)
    seq_in = (normed_seq * gain_in_all).astype(bf16)
    sequence_length = seq_in.shape[0]
    query = dot(seq_in, query_all)
    query_low = rotary_embed(
        query.reshape(sequence_length, local_heads, HEAD_SIZE), sequence_length, 1.0
    ).astype(bf16)
    key_cols = lax.dynamic_slice_in_dim(shared_all, head_group * HEAD_SIZE, HEAD_SIZE, 1)
    value_cols = lax.dynamic_slice_in_dim(
        shared_all, key_value_width + head_group * HEAD_SIZE, HEAD_SIZE, 1
    )
    used_cols = jnp.concatenate(
        [key_cols, value_cols, shared_all[:, 2 * key_value_width :]], axis=1
    )
    shared_projection = dot(seq_in, used_cols)
    keys_reduced = rotary_embed(shared_projection[:, None, :HEAD_SIZE], sequence_length, 1.0)[
        :, 0
    ].astype(bf16)
    values_reduced = shared_projection[:, HEAD_SIZE : 2 * HEAD_SIZE].astype(bf16)
    state_raw = shared_projection[:, 2 * HEAD_SIZE :]
    mixed, log_total = attend(query_low, keys_reduced, values_reduced, QB)
    mixed_low = mixed.astype(bf16)
    gate_z = dot(seq_in, mixer_in_all[:, :channels])
    inner_raw = dot(seq_in, mixer_in_all[:, channels:])
    step_raw = dot(seq_in, step_all)
    (inner, state_in, step_size), mixer_back = jax.vjp(
        mixer_input,
        inner_raw,
        state_raw,
        step_raw,
        filter_inner_f,
        filter_state_all.astype(f32),
        step_bias_f,
    )
    inner_low = inner.astype(bf16)
    state_low = state_in.astype(bf16)

    def scan_piece(inner_v, state_v, step_v, gate_v, decay_v, skip_v):
        return state_scan(inner_v, state_v, step_v, gate_v, decay_v, skip_v, BLK)

    gated, scan_back = jax.vjp(
        scan_piece,
        inner_low.astype(f32),
        state_low.astype(f32),
        step_size,
        gate_z,
        log_decay_f,
        skip_gain_f,
    )
    total_squares = lax.psum(jnp.sum(gated * gated, axis=1), "tensor")
    gated_scale = lax.rsqrt(total_squares / channels_all + epsilon)[:, None]
    gated_norm = gated * gated_scale
    mixer_low = (gated_norm * mixer_gain_f).astype(bf16)

    cut = query_width
    attention_all = second_all[:, :cut]
    mixer_out_all = second_all[:, cut : cut + channels]
    cut += channels
    gate_up_all = second_all[:, cut : cut + 2 * hidden_units]
    cut += 2 * hidden_units
    down_all = second_all[:, cut:]

    mixer_low, back_seq = lax.optimization_barrier((mixer_low, back_seq))
    branch_low = (dot_t(mixed_low, attention_all) + dot_t(mixer_low, mixer_out_all)).astype(bf16)
    hidden = inputs_f + scatter_rows(branch_low)
    scale_post = norm_scale(hidden)
    normed_post = hidden * scale_post
    rows_post_low = (normed_post * gain_post_all).astype(bf16)
    seq_post = gather_rows(rows_post_low)
    gate = dot(seq_post, gate_up_all[:, :hidden_units])
    upper = dot(seq_post, gate_up_all[:, hidden_units:])
    sigmoid_gate = jax.nn.sigmoid(gate)
    silu_gate = gate * sigmoid_gate
    activated_low = (silu_gate * upper).astype(bf16)
    down_low = dot_t(activated_low, down_all).astype(bf16)

    back_act = dot(back_seq, down_all)
    back_gate = back_act * upper * sigmoid_gate * (1.0 + gate * (1.0 - sigmoid_gate))
    back_upper = back_act * silu_gate
    back_gu_low = jnp.concatenate([back_gate, back_upper], axis=1).astype(bf16)
    back_post_low = dot_t(back_gu_low, gate_up_all).astype(bf16)
    back_post = scatter_rows(back_post_low)
    back_down_w = t_dot(back_seq, activated_low).astype(bf16)
    back_gate_up_w = t_dot(seq_post, back_gu_low).astype(bf16)
    back_gain_post = jnp.sum(back_post * normed_post, axis=0)
    back_norm_post = back_post * gain_post_all
    back_hidden = cotangent.astype(f32) + scale_post * (
        back_norm_post - normed_post * jnp.mean(back_norm_post * normed_post, axis=1, keepdims=True)
    )
    back_mix = gather_rows(back_hidden.astype(bf16))

    back_mixer_out_w = t_dot(back_mix, mixer_low).astype(bf16)
    back_attention_w = t_dot(back_mix, mixed_low).astype(bf16)
    early = jnp.concatenate(
        [back_attention_w, back_mixer_out_w, back_gate_up_w, back_down_w], axis=1
    )
    early, back_mix, down_low = lax.optimization_barrier((early, back_mix, down_low))
    tensor_count = lax.axis_size("tensor")
    down_view = down_low.reshape(tensor_count, sequence_length // tensor_count, width)
    down_half = scatter_bits(down_view, "tensor", [1])
    early_rows = lax.psum_scatter(early, "dp", scatter_dimension=0, tiled=True)

    back_norm = dot(back_mix, mixer_out_all)
    back_mixer_gain = jnp.sum(back_norm * gated_norm, axis=0)
    back_scaled = back_norm * mixer_gain_f
    inner_total = lax.psum(jnp.sum(back_scaled * gated_norm, axis=1), "tensor")
    back_gated = gated_scale * (back_scaled - gated_norm * (inner_total / channels_all)[:, None])
    back_inner, back_state, back_step_size, back_gate_z, back_log_decay, back_skip_gain = scan_back(
        back_gated
    )
    (
        back_inner_raw,
        back_state_raw,
        back_step_raw,
        back_filter_inner,
        back_filter_state,
        back_step_bias,
    ) = mixer_back((back_inner, back_state, back_step_size))
    back_mixer_low = jnp.concatenate([back_gate_z, back_inner_raw], axis=1).astype(bf16)
    back_step_low = back_step_raw.astype(bf16)
    back_mixed_low = dot(back_mix, attention_all).astype(bf16)
    mixer_grads = t_dot(seq_in, back_mixer_low).astype(bf16)
    mixer_grads, back_mixed_low, down_half = lax.optimization_barrier(
        (mixer_grads, back_mixed_low, down_half)
    )
    mixer_half = scatter_bits(
        mixer_grads.reshape(dp_count, own_rows, 2 * channels), "dp", [1]
    )
    down_rows = scatter_bits(
        down_half, "tensor", [1 << k for k in range(1, tensor_count.bit_length() - 1)]
    ).reshape(inputs.shape)
    back_query_rot, back_keys_rot, back_values = attend_back(
        query_low, keys_reduced, values_reduced, log_total, back_mixed_low, QB
    )
    back_query_low = (
        rotary_embed(back_query_rot, sequence_length, -1.0)
        .reshape(sequence_length, local_heads * HEAD_SIZE)
        .astype(bf16)
    )
    back_keys = rotary_embed(back_keys_rot[:, None, :], sequence_length, -1.0)[:, 0]
    back_used_low = jnp.concatenate([back_keys, back_values, back_state_raw], axis=1).astype(bf16)
    used_width = back_used_low.shape[1]

    back_query_low, back_used_low, early_rows, down_rows, mixer_half = lax.optimization_barrier(
        (back_query_low, back_used_low, early_rows, down_rows, mixer_half)
    )
    mixer_rows = scatter_bits(
        mixer_half, "dp", [1 << k for k in range(1, dp_count.bit_length() - 1)]
    ).reshape(own_rows, 2 * channels)
    output = (hidden + down_rows).astype(bf16)
    back_in_part = (
        dot_t(back_query_low, query_all)
        + dot_t(back_mixer_low, mixer_in_all)
        + dot_t(back_step_low, step_all)
        + dot_t(back_used_low, used_cols)
    )
    back_gain_in = jnp.sum(back_in_part * normed_seq, axis=0)
    back_in_rows = scatter_rows(back_in_part.astype(bf16))

    spread_state = jnp.pad(
        back_filter_state.reshape(dp_count, filter_rows, filter_columns),
        ((0, 0), (0, own_rows - filter_rows), (0, 0)),
    ).reshape(width, filter_columns)
    back_small = jnp.concatenate(
        [
            t_dot(seq_in, back_step_low),
            back_gain_in[:, None],
            back_gain_post[:, None],
            spread_state,
        ],
        axis=1,
    )
    back_small = jnp.pad(back_small, ((0, 0), (0, small_width - back_small.shape[1])))
    late = jnp.concatenate(
        [
            t_dot(seq_in, back_query_low).astype(bf16),
            t_dot(seq_in, back_used_low).astype(bf16),
            back_small.astype(bf16),
        ],
        axis=1,
    )
    late_rows = scatter_rows(late, "dp")

    cut = query_width
    back_query_w = late_rows[:, :cut]
    used_rows = late_rows[:, cut : cut + used_width].astype(bf16)
    cut += used_width
    small_rows = late_rows[:, cut:]
    back_mixer_in_w = mixer_rows
    back_step_w = small_rows[:, :step_heads]
    select_heads = (jnp.arange(KEY_VALUE_HEADS) == head_group).astype(bf16)
    pair = (
        used_rows[:, : 2 * HEAD_SIZE].reshape(own_rows, 2, 1, HEAD_SIZE)
        * select_heads[None, None, :, None]
    ).reshape(own_rows, 2 * key_value_width)
    common = sum_all(
        jnp.concatenate([pair, used_rows[:, 2 * HEAD_SIZE :], small_rows.astype(bf16)], axis=1), "tensor"
    ).astype(f32)
    back_shared_w = common[:, :shared_width]
    common = common[:, shared_width:]
    back_gain_in = common[:, step_heads]
    back_gain_post = common[:, step_heads + 1]
    back_filter_state = common[:filter_rows, step_heads + 2 : step_heads + 2 + filter_columns]

    cut = query_width
    back_attention_w = early_rows[:, :cut].astype(f32)
    back_mixer_out_w = early_rows[:, cut : cut + channels].astype(f32)
    cut += channels
    back_gate_up_w = early_rows[:, cut : cut + 2 * hidden_units].astype(f32)
    cut += 2 * hidden_units
    back_down_w = early_rows[:, cut:].astype(f32)

    back_norm_in = back_in_rows * gain_in_all
    back_inputs = back_hidden + scale_in * (
        back_norm_in - normed_in * jnp.mean(back_norm_in * normed_in, axis=1, keepdims=True)
    )
    pieces = (back_filter_inner, back_step_bias, back_log_decay, back_skip_gain, back_mixer_gain)
    flat = jnp.concatenate([piece.reshape(-1) for piece in pieces])
    flat = jnp.pad(flat, (0, -flat.shape[0] % 1024))
    flat = sum_all(flat, "dp")
    results = []
    cut = 0
    for piece in pieces:
        results.append(flat[cut : cut + piece.size].reshape(piece.shape))
        cut += piece.size
    back_filter_inner, back_step_bias, back_log_decay, back_skip_gain, back_mixer_gain = results
    return (
        output,
        back_inputs,
        back_gain_in,
        back_query_w,
        back_shared_w,
        back_attention_w,
        back_mixer_in_w.reshape(own_rows, 2, channels),
        back_step_w,
        back_filter_inner,
        back_filter_state,
        back_step_bias,
        back_log_decay,
        back_skip_gain,
        back_mixer_gain,
        back_mixer_out_w,
        back_gain_post,
        back_gate_up_w.reshape(own_rows, 2, hidden_units),
        back_down_w,
    )


def solution(mesh):
    in_specs = (
        P(("dp", "tensor"), None),
        P(("dp", "tensor"), None),
        P("dp"),
        P("dp", "tensor"),
        P("dp", None),
        P("dp", "tensor"),
        P("dp", None, "tensor"),
        P("dp", "tensor"),
        P(None, "tensor"),
        P("dp", None),
        P("tensor"),
        P("tensor"),
        P("tensor"),
        P("tensor"),
        P("dp", "tensor"),
        P("dp"),
        P("dp", None, "tensor"),
        P("dp", "tensor"),
    )
    out_specs = (
        P(("dp", "tensor"), None),
        P(("dp", "tensor"), None),
        P("dp"),
        P("dp", "tensor"),
        P("dp", None),
        P("dp", "tensor"),
        P("dp", None, "tensor"),
        P("dp", "tensor"),
        P(None, "tensor"),
        P("dp", None),
        P("tensor"),
        P("tensor"),
        P("tensor"),
        P("tensor"),
        P("dp", "tensor"),
        P("dp"),
        P("dp", None, "tensor"),
        P("dp", "tensor"),
    )
    return jax.shard_map(body, mesh=mesh, in_specs=in_specs, out_specs=out_specs, check_vma=False)
```
